32 devices in a mesh: row: 2 (over core), col: 16 (over z, y, x).
Axes of the slice: x: 2, y: 2, z: 4, core: 2. Of those that a mesh axis runs over, the one named last changes fastest.
Arguments:
- tokens: bfloat16 [256, 6144], P('row', 'col'), may hold values from -6 to 6
- gate_weight: bfloat16 [6144, 24576], P('row', 'col'), may hold values from -0.15625 to 0.15625
- up_weight: bfloat16 [6144, 24576], P('row', 'col'), may hold values from -0.15625 to 0.15625
- block_mask: int32 [48, 192], P(None, 'col'), may hold values from 0 to 1, as said below
- cotangent: bfloat16 [256, 24576], P('row', 'col'), may hold values from -6 to 6
Outputs:
- hidden: bfloat16 [256, 24576], P('row', 'col')
- input_grad: bfloat16 [256, 6144], P('row', 'col')
- gate_grad: float32 [6144, 24576], P('row', 'col')
- up_grad: float32 [6144, 24576], P('row', 'col')
The draws below stay inside these ranges and needn't reach their ends.
Inputs may be any that keep to these rules, and one draw needn't show every extreme that they name: `block_mask`: in every block column, each run of 24 block rows that starts at a multiple of 24 holds exactly 12 ones, the others zero.
All inputs are finite; a program needn't handle non-finite values.
Results may differ from the reference program's by a relative error of at most 0.0085.
Values may be sent and summed in bfloat16 or wider, within the bound.
No kernel may reach another device: no remote copies, remote signals or barrier semaphores. Data moves between devices by JAX's collectives and lax.ppermute only.
A program may use at most 192 MiB of HBM per device.

```python
import jax
import jax.numpy as jnp
from jax import lax

BLOCK = 128
D = 6144
FF = 24576
TOK_DEV = 128
TOKENS = 256
SEGB = 24


def draw_block_mask(key, part):
    groups = D // BLOCK // SEGB
    scores = jax.random.randint(key, (groups, FF // BLOCK, SEGB), 0, 1 << 20)
    scores = scores * SEGB + jnp.arange(SEGB, dtype=jnp.int32)
    order = jnp.argsort(scores, axis=-1)
    placing = jnp.argsort(order, axis=-1)
    chosen = (placing < SEGB // 2).astype(jnp.int32)
    return jnp.transpose(chosen, (0, 2, 1)).reshape(D // BLOCK, FF // BLOCK)


def strengthened(array, rng, source, target, parts, factor):
    owner, partner = [(jnp.arange(array.shape[position]) // (array.shape[position] // parts)).reshape([-1 if axis == position else 1 for axis in range(array.ndim)]) for position in (source, target)]
    chosen = jax.random.permutation(rng, parts)[partner]
    strong = (owner == chosen) | (owner == (partner + parts // 2) % parts)
    return jnp.where(strong, factor * array, array)


def steps_of(own_key, dims, split, low, top_value):
    def one(position, shards_of):
        steps = jax.random.uniform(jax.random.fold_in(jax.random.fold_in(own_key, 6), position), (shards_of,), jnp.float32, low / len(split), top_value / len(split))
        return jnp.repeat(jnp.exp(steps), dims[position] // shards_of).reshape((-1,) + (1,) * (len(dims) - position - 1))

    factor_of = one(*split[0])
    for cut in split[1:]:
        factor_of = factor_of * one(*cut)
    return factor_of


def centred(rng, extent, spread, most, split=(), kind=jnp.bfloat16):
    drawn = jax.random.normal(rng, extent, jnp.float32) * spread
    if len(split) > 0:
        drawn = steps_of(rng, extent, split, -0.22, 0.18) * drawn
    return jnp.clip(drawn, min=-most, max=most).astype(kind)


def noise_with(key, extent, spread, reach, pieces, heavy, held_as=jnp.bfloat16):
    entries = spread * jax.random.normal(key, extent, jnp.float32)
    if pieces:
        entries = entries * steps_of(key, extent, pieces, -0.22, 0.18)
    return jnp.clip(strengthened(entries, jax.random.fold_in(key, 3), *heavy), -reach, reach).astype(held_as)


def setup_inputs(seed: int = 0) -> dict:
    keys = jax.random.split(jax.random.key(seed), 6)
    tokens = centred(keys[0], (TOKENS, D), 1.0, 6.0, ((0, 2), (1, 16)))
    gate_weight = noise_with(keys[1], (D, FF), (D // 2) ** -0.5, 0.15625, ((0, 2), (1, 16)), (1, 0, 16, 2.0))
    up_weight = noise_with(keys[2], (D, FF), (D // 2) ** -0.5, 0.15625, ((0, 2), (1, 16)), (1, 0, 16, 2.0))
    block_mask = draw_block_mask(jax.random.fold_in(keys[5], 71), 0)
    cotangent = centred(keys[4], (TOKENS, FF), 1.0, 6.0, ((0, 2), (1, 16)))
    return {"tokens": tokens, "gate_weight": gate_weight, "up_weight": up_weight, "block_mask": block_mask, "cotangent": cotangent}


def reference(tokens, gate_weight, up_weight, block_mask, cotangent):
    expanded = jnp.repeat(jnp.repeat(block_mask, BLOCK, axis=0), BLOCK, axis=1).astype(jnp.bfloat16)
    gate_masked = gate_weight * expanded
    up_masked = up_weight * expanded
    gate = jnp.dot(tokens, gate_masked, preferred_element_type=jnp.float32)
    up_values = jnp.dot(tokens, up_masked, preferred_element_type=jnp.float32)
    sig = jax.nn.sigmoid(gate)
    silu_gate = gate * sig
    hidden = (silu_gate * up_values).astype(jnp.bfloat16)
    cot_float = cotangent.astype(jnp.float32)
    grad_gate = (cot_float * up_values * sig * (1.0 + gate * (1.0 - sig))).astype(jnp.bfloat16)
    grad_up = (cot_float * silu_gate).astype(jnp.bfloat16)
    input_grad = (jnp.dot(grad_gate, gate_masked.T, preferred_element_type=jnp.float32)
                  + jnp.dot(grad_up, up_masked.T, preferred_element_type=jnp.float32)).astype(jnp.bfloat16)
    groups = TOKENS // TOK_DEV
    token_groups = tokens.reshape(groups, TOK_DEV, D)
    gate_groups = grad_gate.reshape(groups, TOK_DEV, FF)
    up_groups = grad_up.reshape(groups, TOK_DEV, FF)

    def add_group(running, group_data):
        token_part, gate_slice, up_slice = group_data
        gate_part = lax.dot_general(token_part, gate_slice, (((0,), (0,)), ((), ())), preferred_element_type=jnp.float32).astype(jnp.bfloat16)
        up_part = lax.dot_general(token_part, up_slice, (((0,), (0,)), ((), ())), preferred_element_type=jnp.float32).astype(jnp.bfloat16)
        gate_part = lax.optimization_barrier(gate_part)
        up_part = lax.optimization_barrier(up_part)
        return (running[0] + gate_part.astype(jnp.float32), running[1] + up_part.astype(jnp.float32)), None

    zeros_grad = jnp.zeros((D, FF), jnp.float32)
    totals, unused = lax.scan(add_group, (zeros_grad, zeros_grad), (token_groups, gate_groups, up_groups))
    mask_float = expanded.astype(jnp.float32)
    return hidden, input_grad, totals[0] * mask_float, totals[1] * mask_float
```

```python
import functools

import jax
import jax.numpy as jnp
from jax import lax
from jax.experimental import pallas as pl
from jax.experimental.pallas import tpu as pltpu
from jax.sharding import PartitionSpec as P

BLOCK = 128
MIB = 1 << 20
AXES = ("row", "col")
ROWS, COLS = 2, 16
F32, BF16 = jnp.float32, jnp.bfloat16
VMEM, SMEM = pltpu.VMEM, pltpu.SMEM


def expand_mask(small_mask):
    return jnp.repeat(jnp.repeat(small_mask, BLOCK, axis=0), BLOCK, axis=1)


def general_body(tokens, gate_weight, up_weight, block_mask, cotangent):
    row_groups = lax.axis_size("row")
    row_index = lax.axis_index("row")
    seg_rows = gate_weight.shape[0]
    seg_blocks = seg_rows // BLOCK
    out_columns = gate_weight.shape[1]
    column_blocks = out_columns // BLOCK
    gathered = lax.all_gather(tokens, "col", axis=1, tiled=True)
    mask_groups = block_mask.reshape(row_groups, seg_blocks, column_blocks)
    own_mask = lax.dynamic_index_in_dim(mask_groups, row_index, 0, keepdims=False)
    own_expanded = expand_mask(own_mask).astype(jnp.bfloat16)
    gate_panel, up_panel = (
        lax.all_gather(gate_weight * own_expanded, "row", axis=0, tiled=True),
        lax.all_gather(up_weight * own_expanded, "row", axis=0, tiled=True),
    )
    gate = jnp.dot(gathered, gate_panel, preferred_element_type=jnp.float32)
    up_values = jnp.dot(gathered, up_panel, preferred_element_type=jnp.float32)
    sigmoid_gate = jax.nn.sigmoid(gate)
    silu_gate = gate * sigmoid_gate
    hidden = (silu_gate * up_values).astype(jnp.bfloat16)
    cot_float = cotangent.astype(jnp.float32)
    grad_gate = (cot_float * up_values * sigmoid_gate * (1.0 + gate * (1.0 - sigmoid_gate))).astype(
        jnp.bfloat16
    )
    grad_up = (cot_float * silu_gate).astype(jnp.bfloat16)
    contract = (((1,), (1,)), ((), ()))
    transposed = lax.psum_scatter(
        lax.dot_general(gate_panel, grad_gate, contract, preferred_element_type=jnp.float32)
        + lax.dot_general(up_panel, grad_up, contract, preferred_element_type=jnp.float32),
        "col",
        scatter_dimension=0,
        tiled=True,
    )
    input_grad = transposed.T.astype(jnp.bfloat16)
    token_contract = (((0,), (0,)), ((), ()))
    gate_partial = lax.dot_general(
        gathered, grad_gate, token_contract, preferred_element_type=jnp.float32
    )
    up_partial = lax.dot_general(
        gathered, grad_up, token_contract, preferred_element_type=jnp.float32
    )
    gate_sums, up_sums = (
        lax.psum_scatter(
            gate_partial.astype(jnp.bfloat16), "row", scatter_dimension=0, tiled=True
        ).astype(jnp.float32),
        lax.psum_scatter(
            up_partial.astype(jnp.bfloat16), "row", scatter_dimension=0, tiled=True
        ).astype(jnp.float32),
    )
    mask_float = expand_mask(own_mask).astype(jnp.float32)
    gate_grad = gate_sums * mask_float
    up_grad = up_sums * mask_float
    return (hidden, input_grad, gate_grad, up_grad)


def place(row, z, y, x):
    return row * COLS + z * 4 + y * 2 + x


def z_pairs(k1, k0):
    return [
        (place(k1 ^ (z >> 1), 2 * half + (k0 ^ (z & 1)), y, x), place(half, z, y, x))
        for half in range(2)
        for z in range(4)
        for y in range(2)
        for x in range(2)
    ]


def lane_pairs(first, second):
    return [(r * COLS + c, r * COLS + (c ^ (first, second)[r])) for r in range(2) for c in range(COLS)]


X, Y = 1, 2
NEAR, FAR = lane_pairs(X, Y), lane_pairs(Y, X)
SLACK = 4
SMALL = pl.CostEstimate(flops=1, bytes_accessed=1, transcendentals=0)


def coords():
    row, col = lax.axis_index("row"), lax.axis_index("col")
    return row, col // 4, (col // 2) % 2, col % 2


def flip(bit, with_bit):
    return bit + with_bit - 2 * bit * with_bit


def block_of(q, dnear, dfar, k1, k0):
    row, z, y, x = q
    dy = dnear * row + dfar * (1 - row)
    dx = dnear * (1 - row) + dfar * row
    return flip(k0, z % 2) * 4 + flip(dy, y) * 2 + flip(dx, x), flip(k1, z // 2)


def in_vmem(array):
    return pltpu.with_memory_space_constraint(array, VMEM)


def in_hbm(array):
    return pltpu.with_memory_space_constraint(array, pltpu.HBM)


def spec(space):
    return pl.BlockSpec(memory_space=space)


def spanning(index):
    return pl.ds(pl.multiple_of(index * BLOCK, BLOCK), BLOCK)


def kept_of(listed):
    return listed.shape[1] // 2 - SLACK


def list_kernel(mask, listed):
    columns, half = listed.shape[0], listed.shape[1] // 2
    segs = mask.shape[1] // ROWS
    low = lax.axis_index("row") == 0
    own = jnp.where(low, mask[:, :segs], mask[:, segs:])
    before = lax.broadcasted_iota(jnp.int32, (segs, segs), 0) <= lax.broadcasted_iota(jnp.int32, (segs, segs), 1)
    kept = jnp.dot(own.astype(F32), before.astype(F32), preferred_element_type=F32).astype(jnp.int32)
    dropped = lax.broadcasted_iota(jnp.int32, (columns, segs), 1) + 1 - kept
    lane = lax.broadcasted_iota(jnp.int32, (columns, 2 * half), 1)
    out = jnp.zeros((columns, 2 * half), jnp.int32)
    for counts, first in ((kept, 0), (dropped, half)):
        for k in range(segs // 2):
            place = jnp.sum((counts <= k).astype(jnp.int32), axis=1, keepdims=True)
            out = jnp.where(lane == first + k, place, out)
    listed[...] = out


def places(mask_t, segs):
    return pl.pallas_call(
        list_kernel,
        out_shape=VMEM((mask_t.shape[0], segs + 2 * SLACK), jnp.int32),
        in_specs=[spec(VMEM)],
        out_specs=spec(VMEM),
        compiler_params=pltpu.CompilerParams(vmem_limit_bytes=4 * MIB),
        cost_estimate=SMALL,
        name="places",
    )(mask_t)


def pack_kernel(first, turning, listed, gate_w, up_w, *refs):
    if turning:
        earlier, _, packed, turned, sem = refs
    else:
        _, packed, sem = refs
    columns, kept = packed.shape[0], kept_of(listed)

    def column(j, _):
        cols = spanning(first + j)
        for k in range(kept):
            rows = spanning(listed[first + j, k])
            to = packed.at[j, k * BLOCK : (k + 1) * BLOCK]
            pltpu.make_async_copy(gate_w.at[rows, cols], to.at[:, :BLOCK], sem).start()
            pltpu.make_async_copy(up_w.at[rows, cols], to.at[:, BLOCK:], sem).start()
        return 0

    lax.fori_loop(0, columns, column, 0)
    if turning:

        def turn(j, _):
            turned[j] = earlier[j].T
            return 0

        lax.fori_loop(0, earlier.shape[0], turn, 0)
    pltpu.make_async_copy(packed, packed, sem).wait()


def pack(first, columns, listed, gate_w, up_w, later_than, earlier=None):
    turning = earlier is not None
    outs = [VMEM((columns, kept_of(listed) * BLOCK, 2 * BLOCK), BF16)]
    if turning:
        outs.append(VMEM((earlier.shape[0], earlier.shape[2], earlier.shape[1]), BF16))
    return pl.pallas_call(
        functools.partial(pack_kernel, first, turning),
        out_shape=outs,
        in_specs=[spec(SMEM), spec(pltpu.HBM), spec(pltpu.HBM)] + [spec(VMEM)] * turning + [spec(pl.ANY)],
        out_specs=[spec(VMEM)] * len(outs),
        scratch_shapes=[pltpu.SemaphoreType.DMA],
        compiler_params=pltpu.CompilerParams(vmem_limit_bytes=4 * MIB),
        cost_estimate=SMALL,
        name="pack",
    )(listed, in_hbm(gate_w), in_hbm(up_w), *([in_vmem(earlier)] if turning else []), later_than)


def forward_kernel(turn, listed, packed_a, packed_b, own, near, far, both, part, turned, tokens):
    q = coords()
    width = own.shape[1] // BLOCK
    for ref, dnear, dfar in ((own, 0, 0), (near, 1, 0), (far, 0, 1), (both, 1, 1)):
        for k0 in range(2):
            chip, _ = block_of(q, dnear, dfar, turn, k0)
            for s in range(width):
                tokens[chip * width + s] = ref[k0 * BLOCK : (k0 + 1) * BLOCK, s * BLOCK : (s + 1) * BLOCK]
    cut = packed_a.shape[0]
    for j in range(part.shape[0]):
        picked = jnp.concatenate([tokens[listed[j, k]] for k in range(kept_of(listed))], axis=1)
        weights = packed_a[j] if j < cut else packed_b[j - cut]
        part[j] = jnp.dot(picked, weights, preferred_element_type=F32)
    for i in range(tokens.shape[0]):
        turned[i] = tokens[i].T


def forward(turn, listed, packed, parts):
    columns = packed[0].shape[0] + packed[1].shape[0]
    seg = parts[0].shape[1] // BLOCK * 8
    return pl.pallas_call(
        functools.partial(forward_kernel, turn),
        out_shape=[VMEM((columns, BLOCK, 2 * BLOCK), F32), VMEM((seg, BLOCK, BLOCK), BF16)],
        in_specs=[spec(SMEM)] + [spec(VMEM)] * 6,
        out_specs=[spec(VMEM)] * 2,
        scratch_shapes=[VMEM((seg, BLOCK, BLOCK), BF16)],
        compiler_params=pltpu.CompilerParams(vmem_limit_bytes=8 * MIB),
        cost_estimate=SMALL,
        name="forward",
    )(listed, *map(in_vmem, packed), *parts)


def backward_kernel(
    turn, listed, turned_a, packed_b, part, other, cot, other_cot, *rest
):
    if turn:
        before, gate_in, up_in, hidden, grads, s00, s01, s10, s11, gate_out, up_out, acc, zeros, sem = rest
    else:
        hidden, grads, s00, s01, s10, s11, gate_out, up_out, acc, zeros, sem = rest
    q = coords()
    columns, kept = part.shape[0], kept_of(listed)
    mine = flip(turn, q[1] // 2) == q[0]
    acc[...] = jnp.zeros_like(acc)
    zeros[...] = jnp.zeros_like(zeros)
    cut = turned_a.shape[0]

    def column(j, packed, at):
        cols = spanning(j)
        total = part[j] + other[j]
        gate, up = total[:, :BLOCK], total[:, BLOCK:]
        sig = 1.0 / (1.0 + jnp.exp(-gate))
        silu = gate * sig
        cotf = jnp.where(mine, cot[:, cols], other_cot[:, cols]).astype(F32)
        shown = (silu * up).astype(BF16)
        hidden[:, cols] = jnp.where(mine, shown, before[:, cols]) if turn else shown
        grads[j, :, :BLOCK] = (cotf * up * sig * (1.0 + gate * (1.0 - sig))).astype(BF16)
        grads[j, :, BLOCK:] = (cotf * silu).astype(BF16)
        facing = (((1,), (0 if packed is turned_a else 1,)), ((), ()))
        spread = lax.dot_general(grads[j], packed[at], facing, preferred_element_type=F32)
        for k in range(kept):
            acc[listed[j, k]] += spread[:, k * BLOCK : (k + 1) * BLOCK]

    def clear(j):
        for k in range(kept):
            rows = spanning(listed[j, kept + SLACK + k])
            pltpu.make_async_copy(zeros, gate_out.at[rows, spanning(j)], sem).start()
            pltpu.make_async_copy(zeros, up_out.at[rows, spanning(j)], sem).start()

    cleared = columns // 2
    lax.fori_loop(0, cleared, lambda j, _: (clear(turn * cleared + j), 0)[1], 0)
    step = 3
    for packed, first, number in ((turned_a, 0, cut), (packed_b, cut, columns - cut)):

        def steps(g, _, packed=packed, first=first):
            for u in range(step):
                column(first + g * step + u, packed, g * step + u)
            return 0

        lax.fori_loop(0, number // step, steps, 0)
    width = s00.shape[1] // BLOCK
    for ref, dnear, dfar in ((s11, 1, 1), (s01, 0, 1), (s10, 1, 0), (s00, 0, 0)):
        for k0 in range(2):
            chip, _ = block_of(q, dnear, dfar, turn, k0)
            for s in range(width):
                ref[k0 * BLOCK : (k0 + 1) * BLOCK, s * BLOCK : (s + 1) * BLOCK] = acc[chip * width + s].astype(BF16)
    part_written = gate_out.at[:, pl.ds(0, cleared * BLOCK)]
    pltpu.make_async_copy(part_written, part_written, sem).wait()


def backward(turn, listed, packed, part, other, cot, other_cot, width, grad_shape, before=None):
    columns = part.shape[0]
    extra = [] if before is None else [before[0], in_hbm(before[1]), in_hbm(before[2])]
    return pl.pallas_call(
        functools.partial(backward_kernel, turn),
        out_shape=[VMEM(cot.shape, BF16), VMEM((columns, BLOCK, 2 * BLOCK), BF16)]
        + [VMEM((2 * BLOCK, width), BF16)] * 4
        + [pltpu.HBM(grad_shape, F32)] * 2,
        in_specs=[spec(SMEM)] + [spec(VMEM)] * 6 + ([spec(VMEM)] + [spec(pltpu.HBM)] * 2 if extra else []),
        out_specs=[spec(VMEM)] * 6 + [spec(pltpu.HBM)] * 2,
        scratch_shapes=[
            VMEM((8 * width // BLOCK, BLOCK, BLOCK), F32),
            VMEM((BLOCK, BLOCK), F32),
            pltpu.SemaphoreType.DMA,
        ],
        input_output_aliases={8: 6, 9: 7} if extra else {},
        compiler_params=pltpu.CompilerParams(vmem_limit_bytes=8 * MIB),
        cost_estimate=SMALL,
        name="backward",
    )(listed, *map(in_vmem, packed), in_vmem(part), in_vmem(other), cot, other_cot, *extra)


def weight_kernel(first, listed, toks0, toks1, grads0, grads1, gate_in, up_in, _, gate_out, up_out, token, stage, sem):
    kept = kept_of(listed)
    for slot in range(stage.shape[0]):
        j = first + slot
        picked = jnp.concatenate(
            [jnp.concatenate([toks0[listed[j, k]], toks1[listed[j, k]]], axis=1) for k in range(kept)], axis=0
        )
        grads = jnp.concatenate([grads0[j], grads1[j]], axis=0)
        stage[slot] = jnp.dot(picked, grads, preferred_element_type=F32)
        for k in range(kept):
            rows = spanning(listed[j, k])
            here = stage.at[slot, k * BLOCK : (k + 1) * BLOCK]
            pltpu.make_async_copy(here.at[:, :BLOCK], gate_out.at[rows, spanning(j)], sem).start()
            pltpu.make_async_copy(here.at[:, BLOCK:], up_out.at[rows, spanning(j)], sem).start()
    token[...] = jnp.zeros_like(token)
    pltpu.make_async_copy(stage, stage, sem).wait()


def weight_grads(first, count, listed, tokens, grads, written, later_than):
    kept = kept_of(listed)
    grad = pltpu.HBM(written[0].shape, F32)
    return pl.pallas_call(
        functools.partial(weight_kernel, first),
        out_shape=[grad, grad, VMEM((8, BLOCK), F32)],
        in_specs=[spec(SMEM)] + [spec(VMEM)] * 4 + [spec(pltpu.HBM)] * 2 + [spec(pl.ANY)],
        out_specs=[spec(pltpu.HBM)] * 2 + [spec(VMEM)],
        scratch_shapes=[VMEM((count, kept * BLOCK, 2 * BLOCK), F32), pltpu.SemaphoreType.DMA],
        input_output_aliases={5: 0, 6: 1},
        compiler_params=pltpu.CompilerParams(vmem_limit_bytes=12 * MIB),
        cost_estimate=SMALL,
        name="weight_grads",
    )(listed, *map(in_vmem, tokens), *map(in_vmem, grads), in_hbm(written[0]), in_hbm(written[1]), later_than)


def add_kernel(*refs):
    out = refs[-1]
    total = refs[0][...].astype(F32)
    for ref in refs[1:-2]:
        total += ref[...].astype(F32)
    out[...] = total.astype(BF16)


def add(*terms, later_than):
    return pl.pallas_call(
        add_kernel,
        out_shape=VMEM(terms[0].shape, BF16),
        in_specs=[spec(VMEM)] * len(terms) + [spec(pl.ANY)],
        out_specs=spec(VMEM),
        compiler_params=pltpu.CompilerParams(vmem_limit_bytes=4 * MIB),
        cost_estimate=SMALL,
        name="add",
    )(*terms, later_than)


def chip_body(tokens, gate_weight, up_weight, block_mask, cotangent):
    swap = [(0, 1), (1, 0)]
    width = tokens.shape[1]
    columns, segs = gate_weight.shape[1] // BLOCK, gate_weight.shape[0] // BLOCK
    cut = columns // 2
    other_cot = lax.ppermute(cotangent, "row", swap)
    listed = places(block_mask.T, segs)

    def gathered(turn):
        return jnp.concatenate([lax.ppermute(tokens, AXES, z_pairs(turn, k0)) for k0 in range(2)], axis=0)

    owns = [gathered(0), gathered(1)]
    nears = [lax.ppermute(own, AXES, NEAR) for own in owns]
    fars = [lax.ppermute(own, AXES, FAR) for own in owns]
    (pack_a,) = pack(0, cut, listed, gate_weight, up_weight, owns[1])
    pack_b, turned_a = pack(cut, columns - cut, listed, gate_weight, up_weight, nears[1], pack_a)
    boths = [lax.ppermute(near, AXES, FAR) for near in nears]
    held = list(zip(owns, nears, fars, boths))

    parts, toks = zip(*[forward(turn, listed, (pack_a, pack_b), held[turn]) for turn in range(2)])
    others = [lax.ppermute(part, "row", swap) for part in parts]
    done = []
    for turn in range(2):
        before = (done[0][0], done[0][6], done[0][7]) if turn else None
        weights = (turned_a, pack_b)
        done.append(
            backward(
                turn, listed, weights, parts[turn], others[turn], cotangent, other_cot, width, gate_weight.shape, before
            )
        )
    grads = [out[1] for out in done]
    hidden = done[1][0]

    (a00, a01, a10, a11), (b00, b01, b10, b11) = done[0][2:6], done[1][2:6]
    first_a, direct_a = lax.ppermute(a11, AXES, FAR), lax.ppermute(a01, AXES, FAR)
    first_b, direct_b = lax.ppermute(b11, AXES, FAR), lax.ppermute(b01, AXES, FAR)
    sum_a = add(a10, first_a, later_than=b10)
    carried_a = lax.ppermute(sum_a, AXES, NEAR)
    lead, middle = columns // 3, columns // 4
    written = done[1][6:8]
    *written, token = weight_grads(0, lead, listed, toks, grads, written, sum_a)
    sum_b = add(b10, first_b, later_than=token)
    carried_b = lax.ppermute(sum_b, AXES, NEAR)
    here_a = add(a00, direct_a, carried_a, later_than=sum_b)
    *written, token = weight_grads(lead, middle, listed, toks, grads, written, here_a)
    here_b = add(b00, direct_b, carried_b, later_than=token)
    total = jnp.zeros(tokens.shape, F32)
    for turn, here in enumerate((here_a, here_b)):
        for k0 in range(2):
            back = [(b, a) for a, b in z_pairs(turn, k0)]
            total += lax.ppermute(here[k0 * BLOCK : (k0 + 1) * BLOCK], AXES, back).astype(F32)
    input_grad = total.astype(BF16)
    last = lead + middle
    *written, token = weight_grads(last, columns - last, listed, toks, grads, written, here_b)
    return hidden, input_grad, *written


def solution(mesh):
    fits = mesh.shape["row"] == ROWS and mesh.shape["col"] == COLS
    placed = (P("row", "col"), P("row", "col"), P("row", "col"), P(None, "col"), P("row", "col"))
    return jax.shard_map(
        chip_body if fits else general_body,
        mesh=mesh,
        in_specs=placed,
        out_specs=(P("row", "col"), P("row", "col"), P("row", "col"), P("row", "col")),
        check_vma=False,
    )
```

```python
import functools

import jax
import jax.numpy as jnp
from jax import lax
from jax.experimental import pallas as pl
from jax.experimental.pallas import tpu as pltpu
from jax.sharding import PartitionSpec as P

BLOCK = 128
MIB = 1 << 20
AXES = ("row", "col")
ROWS, COLS = 2, 16
F32, BF16 = jnp.float32, jnp.bfloat16
VMEM, SMEM = pltpu.VMEM, pltpu.SMEM


def expand_mask(small_mask):
    return jnp.repeat(jnp.repeat(small_mask, BLOCK, axis=0), BLOCK, axis=1)


def general_body(tokens, gate_weight, up_weight, block_mask, cotangent):
    row_groups = lax.axis_size("row")
    row_index = lax.axis_index("row")
    seg_rows = gate_weight.shape[0]
    seg_blocks = seg_rows // BLOCK
    out_columns = gate_weight.shape[1]
    column_blocks = out_columns // BLOCK
    gathered = lax.all_gather(tokens, "col", axis=1, tiled=True)
    mask_groups = block_mask.reshape(row_groups, seg_blocks, column_blocks)
    own_mask = lax.dynamic_index_in_dim(mask_groups, row_index, 0, keepdims=False)
    own_expanded = expand_mask(own_mask).astype(jnp.bfloat16)
    gate_panel, up_panel = (
        lax.all_gather(gate_weight * own_expanded, "row", axis=0, tiled=True),
        lax.all_gather(up_weight * own_expanded, "row", axis=0, tiled=True),
    )
    gate = jnp.dot(gathered, gate_panel, preferred_element_type=jnp.float32)
    up_values = jnp.dot(gathered, up_panel, preferred_element_type=jnp.float32)
    sigmoid_gate = jax.nn.sigmoid(gate)
    silu_gate = gate * sigmoid_gate
    hidden = (silu_gate * up_values).astype(jnp.bfloat16)
    cot_float = cotangent.astype(jnp.float32)
    grad_gate = (cot_float * up_values * sigmoid_gate * (1.0 + gate * (1.0 - sigmoid_gate))).astype(
        jnp.bfloat16
    )
    grad_up = (cot_float * silu_gate).astype(jnp.bfloat16)
    contract = (((1,), (1,)), ((), ()))
    transposed = lax.psum_scatter(
        lax.dot_general(gate_panel, grad_gate, contract, preferred_element_type=jnp.float32)
        + lax.dot_general(up_panel, grad_up, contract, preferred_element_type=jnp.float32),
        "col",
        scatter_dimension=0,
        tiled=True,
    )
    input_grad = transposed.T.astype(jnp.bfloat16)
    token_contract = (((0,), (0,)), ((), ()))
    gate_partial = lax.dot_general(
        gathered, grad_gate, token_contract, preferred_element_type=jnp.float32
    )
    up_partial = lax.dot_general(
        gathered, grad_up, token_contract, preferred_element_type=jnp.float32
    )
    gate_sums, up_sums = (
        lax.psum_scatter(
            gate_partial.astype(jnp.bfloat16), "row", scatter_dimension=0, tiled=True
        ).astype(jnp.float32),
        lax.psum_scatter(
            up_partial.astype(jnp.bfloat16), "row", scatter_dimension=0, tiled=True
        ).astype(jnp.float32),
    )
    mask_float = expand_mask(own_mask).astype(jnp.float32)
    gate_grad = gate_sums * mask_float
    up_grad = up_sums * mask_float
    return (hidden, input_grad, gate_grad, up_grad)


def place(row, z, y, x):
    return row * COLS + z * 4 + y * 2 + x


def z_pairs(k1, k0):
    return [
        (place(k1 ^ (z >> 1), 2 * half + 1 - (k0 ^ (z & 1)), y, x), place(half, z, y, x))
        for half in range(2)
        for z in range(4)
        for y in range(2)
        for x in range(2)
    ]


def lane_pairs(first, second):
    return [(r * COLS + c, r * COLS + (c ^ (first, second)[r])) for r in range(2) for c in range(COLS)]


X, Y = 1, 2
NEAR, FAR, ACROSS = lane_pairs(X, Y), lane_pairs(Y, X), lane_pairs(X + Y, X + Y)
SLACK = 4
SMALL = pl.CostEstimate(flops=1, bytes_accessed=1, transcendentals=0)


def coords():
    row, col = lax.axis_index("row"), lax.axis_index("col")
    return row, col // 4, (col // 2) % 2, col % 2


def flip(bit, with_bit):
    return bit + with_bit - 2 * bit * with_bit


def block_of(q, dnear, dfar, k1, k0):
    row, z, y, x = q
    dy = dnear * row + dfar * (1 - row)
    dx = dnear * (1 - row) + dfar * row
    return flip(1 - k0, z % 2) * 4 + flip(dy, y) * 2 + flip(dx, x), flip(k1, z // 2)


def in_vmem(array):
    return pltpu.with_memory_space_constraint(array, VMEM)


def in_hbm(array):
    return pltpu.with_memory_space_constraint(array, pltpu.HBM)


def spec(space):
    return pl.BlockSpec(memory_space=space)


def spanning(index):
    return pl.ds(pl.multiple_of(index * BLOCK, BLOCK), BLOCK)


def kept_of(listed):
    return listed.shape[1] // 2 - SLACK


def list_kernel(mask, listed):
    columns, half = listed.shape[0], listed.shape[1] // 2
    segs = mask.shape[1] // ROWS
    low = lax.axis_index("row") == 0
    own = jnp.where(low, mask[:, :segs], mask[:, segs:])
    before = lax.broadcasted_iota(jnp.int32, (segs, segs), 0) <= lax.broadcasted_iota(jnp.int32, (segs, segs), 1)
    kept = jnp.dot(own.astype(F32), before.astype(F32), preferred_element_type=F32).astype(jnp.int32)
    dropped = lax.broadcasted_iota(jnp.int32, (columns, segs), 1) + 1 - kept
    lane = lax.broadcasted_iota(jnp.int32, (columns, 2 * half), 1)
    out = jnp.zeros((columns, 2 * half), jnp.int32)
    for counts, first in ((kept, 0), (dropped, half)):
        for k in range(segs // 2):
            place = jnp.sum((counts <= k).astype(jnp.int32), axis=1, keepdims=True)
            out = jnp.where(lane == first + k, place, out)
    listed[...] = out


def places(mask_t, segs):
    return pl.pallas_call(
        list_kernel,
        out_shape=VMEM((mask_t.shape[0], segs + 2 * SLACK), jnp.int32),
        in_specs=[spec(VMEM)],
        out_specs=spec(VMEM),
        compiler_params=pltpu.CompilerParams(vmem_limit_bytes=4 * MIB),
        cost_estimate=SMALL,
        name="places",
    )(mask_t)


def pack_kernel(first, turning, listed, gate_w, up_w, *refs):
    if turning:
        earlier, _, packed, turned, sem = refs
    else:
        _, packed, sem = refs
    columns, kept = packed.shape[0], kept_of(listed)

    def column(j, _):
        cols = spanning(first + j)
        for k in range(kept):
            rows = spanning(listed[first + j, k])
            to = packed.at[j, k * BLOCK : (k + 1) * BLOCK]
            pltpu.make_async_copy(gate_w.at[rows, cols], to.at[:, :BLOCK], sem).start()
            pltpu.make_async_copy(up_w.at[rows, cols], to.at[:, BLOCK:], sem).start()
        return 0

    lax.fori_loop(0, columns, column, 0)
    if turning:

        def turn(j, _):
            turned[j] = earlier[j].T
            return 0

        lax.fori_loop(0, earlier.shape[0], turn, 0)
    pltpu.make_async_copy(packed, packed, sem).wait()


def pack(first, columns, listed, gate_w, up_w, later_than, earlier=None):
    turning = earlier is not None
    outs = [VMEM((columns, kept_of(listed) * BLOCK, 2 * BLOCK), BF16)]
    if turning:
        outs.append(VMEM((earlier.shape[0], earlier.shape[2], earlier.shape[1]), BF16))
    return pl.pallas_call(
        functools.partial(pack_kernel, first, turning),
        out_shape=outs,
        in_specs=[spec(SMEM), spec(pltpu.HBM), spec(pltpu.HBM)] + [spec(VMEM)] * turning + [spec(pl.ANY)],
        out_specs=[spec(VMEM)] * len(outs),
        scratch_shapes=[pltpu.SemaphoreType.DMA],
        compiler_params=pltpu.CompilerParams(vmem_limit_bytes=4 * MIB),
        cost_estimate=SMALL,
        name="pack",
    )(listed, in_hbm(gate_w), in_hbm(up_w), *([in_vmem(earlier)] if turning else []), later_than)


def start_clearing(first, count, listed, zeros, gate_out, up_out, sem):
    zeros[...] = jnp.zeros_like(zeros)
    kept = kept_of(listed)

    def column(j, _):
        cols = spanning(first + j)
        for k in range(kept):
            rows = spanning(listed[first + j, kept + SLACK + k])
            pltpu.make_async_copy(zeros, gate_out.at[rows, cols], sem).start()
            pltpu.make_async_copy(zeros, up_out.at[rows, cols], sem).start()
        return 0

    lax.fori_loop(0, count, column, 0)


def finish_clearing(count, gate_out, sem):
    written = gate_out.at[:, pl.ds(0, count * BLOCK)]
    pltpu.make_async_copy(written, written, sem).wait()


CLEARING = [VMEM((BLOCK, BLOCK), F32), pltpu.SemaphoreType.DMA]


def forward_kernel(turn, listed, packed_a, packed_b, here, there, _, part, turned, tokens):
    q = coords()
    width = here.shape[1] // BLOCK
    for dfar, ref in enumerate((here, there)):
        for slot in range(4):
            chip, _ = block_of(q, slot // 2, dfar, turn, slot % 2)
            for s in range(width):
                tokens[chip * width + s] = ref[slot * BLOCK : (slot + 1) * BLOCK, s * BLOCK : (s + 1) * BLOCK]
    cut = packed_a.shape[0]
    for j in range(part.shape[0]):
        picked = jnp.concatenate([tokens[listed[j, k]] for k in range(kept_of(listed))], axis=1)
        weights = packed_a[j] if j < cut else packed_b[j - cut]
        part[j] = jnp.dot(picked, weights, preferred_element_type=F32)
    for i in range(tokens.shape[0]):
        turned[i] = tokens[i].T


def forward(turn, listed, packed, parts, later_than):
    columns = packed[0].shape[0] + packed[1].shape[0]
    seg = parts[0].shape[1] // BLOCK * 8
    return pl.pallas_call(
        functools.partial(forward_kernel, turn),
        out_shape=[VMEM((columns, BLOCK, 2 * BLOCK), F32), VMEM((seg, BLOCK, BLOCK), BF16)],
        in_specs=[spec(SMEM)] + [spec(VMEM)] * 4 + [spec(pl.ANY)],
        out_specs=[spec(VMEM)] * 2,
        scratch_shapes=[VMEM((seg, BLOCK, BLOCK), BF16)],
        compiler_params=pltpu.CompilerParams(vmem_limit_bytes=8 * MIB),
        cost_estimate=SMALL,
        name="forward",
    )(listed, *map(in_vmem, packed), *parts, later_than)


def backward_kernel(turn, listed, turned_a, turned_b, part, other, cot, other_cot, *refs):
    if turn:
        before, hidden, grads, far, near, acc = refs
    else:
        hidden, grads, far, near, acc = refs
    q = coords()
    columns, kept = part.shape[0], kept_of(listed)
    mine = flip(turn, q[1] // 2) == q[0]
    acc[...] = jnp.zeros_like(acc)
    cut = turned_a.shape[0]

    def column(j, turned, at):
        cols = spanning(j)
        total = part[j] + other[j]
        gate, up = total[:, :BLOCK], total[:, BLOCK:]
        sig = 1.0 / (1.0 + jnp.exp(-gate))
        silu = gate * sig
        cotf = jnp.where(mine, cot[:, cols], other_cot[:, cols]).astype(F32)
        shown = (silu * up).astype(BF16)
        hidden[:, cols] = jnp.where(mine, shown, before[:, cols]) if turn else shown
        grads[j, :, :BLOCK] = (cotf * up * sig * (1.0 + gate * (1.0 - sig))).astype(BF16)
        grads[j, :, BLOCK:] = (cotf * silu).astype(BF16)
        spread = jnp.dot(grads[j], turned[at], preferred_element_type=F32)
        for k in range(kept):
            acc[listed[j, k]] += spread[:, k * BLOCK : (k + 1) * BLOCK]

    step = 3
    for turned, first, number in ((turned_a, 0, cut), (turned_b, cut, columns - cut)):

        def steps(g, _, turned=turned, first=first):
            for u in range(step):
                column(first + g * step + u, turned, g * step + u)
            return 0

        lax.fori_loop(0, number // step, steps, 0)
    width = far.shape[1] // BLOCK
    for dfar, ref in enumerate((near, far)):
        for slot in range(4):
            chip, _ = block_of(q, 1 - slot // 2, dfar, turn, slot % 2)
            for s in range(width):
                ref[slot * BLOCK : (slot + 1) * BLOCK, s * BLOCK : (s + 1) * BLOCK] = acc[chip * width + s].astype(BF16)


def backward(turn, listed, packed, part, other, cot, other_cot, width, before=None):
    columns = part.shape[0]
    extra = [] if before is None else [before]
    return pl.pallas_call(
        functools.partial(backward_kernel, turn),
        out_shape=[VMEM(cot.shape, BF16), VMEM((columns, BLOCK, 2 * BLOCK), BF16)]
        + [VMEM((4 * BLOCK, width), BF16)] * 2,
        in_specs=[spec(SMEM)] + [spec(VMEM)] * (6 + len(extra)),
        out_specs=[spec(VMEM)] * 4,
        scratch_shapes=[VMEM((8 * width // BLOCK, BLOCK, BLOCK), F32)],
        compiler_params=pltpu.CompilerParams(vmem_limit_bytes=8 * MIB),
        cost_estimate=SMALL,
        name="backward",
    )(listed, *map(in_vmem, packed), in_vmem(part), in_vmem(other), cot, other_cot, *extra)


def weight_kernel(first, count, listed, toks0, toks1, grads0, grads1, gate_in, up_in, _, gate_out, up_out, stage, sems):
    kept, slots = kept_of(listed), stage.shape[0]
    for j in range(first, first + count):
        slot = (j - first) % slots
        if j - first >= slots:
            pltpu.make_async_copy(stage.at[slot], stage.at[slot], sems.at[slot]).wait()
        picked = jnp.concatenate(
            [jnp.concatenate([toks0[listed[j, k]], toks1[listed[j, k]]], axis=1) for k in range(kept)], axis=0
        )
        grads = jnp.concatenate([grads0[j], grads1[j]], axis=0)
        stage[slot] = jnp.dot(picked, grads, preferred_element_type=F32)
        for k in range(kept):
            rows = spanning(listed[j, k])
            here = stage.at[slot, k * BLOCK : (k + 1) * BLOCK]
            pltpu.make_async_copy(here.at[:, :BLOCK], gate_out.at[rows, spanning(j)], sems.at[slot]).start()
            pltpu.make_async_copy(here.at[:, BLOCK:], up_out.at[rows, spanning(j)], sems.at[slot]).start()
    for slot in range(slots):
        pltpu.make_async_copy(stage.at[slot], stage.at[slot], sems.at[slot]).wait()


def weight_grads(first, count, listed, tokens, grads, written, later_than):
    slots = min(6, count)
    return pl.pallas_call(
        functools.partial(weight_kernel, first, count),
        out_shape=[pltpu.HBM(grad.shape, F32) for grad in written],
        in_specs=[spec(SMEM)] + [spec(VMEM)] * 4 + [spec(pltpu.HBM)] * 2 + [spec(pl.ANY)],
        out_specs=[spec(pltpu.HBM)] * 2,
        scratch_shapes=[VMEM((slots, kept_of(listed) * BLOCK, 2 * BLOCK), F32), pltpu.SemaphoreType.DMA((slots,))],
        input_output_aliases={5: 0, 6: 1},
        compiler_params=pltpu.CompilerParams(vmem_limit_bytes=16 * MIB),
        cost_estimate=SMALL,
        name="weight_grads",
    )(listed, *map(in_vmem, tokens), *map(in_vmem, grads), *map(in_hbm, written), later_than)


def add_kernel(firsts, *refs):
    out = refs[-1]
    total = 0.0
    for first, ref in zip(firsts, refs):
        total += ref[first : first + out.shape[0]].astype(F32)
    out[...] = total.astype(BF16)


def add(*terms, later_than):
    firsts, arrays = zip(*terms)
    return pl.pallas_call(
        functools.partial(add_kernel, firsts),
        out_shape=VMEM((2 * BLOCK, arrays[0].shape[1]), BF16),
        in_specs=[spec(VMEM)] * len(arrays) + [spec(pl.ANY)],
        out_specs=spec(VMEM),
        compiler_params=pltpu.CompilerParams(vmem_limit_bytes=4 * MIB),
        cost_estimate=SMALL,
        name="add",
    )(*arrays, later_than)


def join_kernel(_, *refs):
    ins, out = refs[:-1], refs[-1]
    size = ins[0].shape[0]
    for i, ref in enumerate(ins):
        out[i * size : (i + 1) * size] = ref[...]


def join(*parts, later_than):
    rows, width = parts[0].shape
    return pl.pallas_call(
        join_kernel,
        out_shape=VMEM((len(parts) * rows, width), BF16),
        in_specs=[spec(pl.ANY)] + [spec(VMEM)] * len(parts),
        out_specs=spec(VMEM),
        compiler_params=pltpu.CompilerParams(vmem_limit_bytes=4 * MIB),
        cost_estimate=SMALL,
        name="join",
    )(later_than, *parts)


def mix_kernel(_, own, near, *outs):
    half = own.shape[0] // 2
    for i, out in enumerate(outs):
        out[:half] = own[i * half : (i + 1) * half]
        out[half:] = near[i * half : (i + 1) * half]


def mix(own, near, later_than):
    return pl.pallas_call(
        mix_kernel,
        out_shape=[VMEM(own.shape, BF16)] * 2,
        in_specs=[spec(pl.ANY)] + [spec(VMEM)] * 2,
        out_specs=[spec(VMEM)] * 2,
        compiler_params=pltpu.CompilerParams(vmem_limit_bytes=4 * MIB),
        cost_estimate=SMALL,
        name="mix",
    )(later_than, own, near)


def turn_kernel(listed, packed, _, turned, gate_out, up_out, zeros, sem):
    start_clearing(0, listed.shape[0], listed, zeros, gate_out, up_out, sem)

    def turn(j, _):
        turned[j] = packed[j].T
        return 0

    lax.fori_loop(0, packed.shape[0], turn, 0)
    finish_clearing(listed.shape[0], gate_out, sem)


def transposed(listed, packed, grad_shape, later_than):
    columns, rows, wide = packed.shape
    return pl.pallas_call(
        turn_kernel,
        out_shape=[VMEM((columns, wide, rows), BF16)] + [pltpu.HBM(grad_shape, F32)] * 2,
        in_specs=[spec(SMEM), spec(VMEM), spec(pl.ANY)],
        out_specs=[spec(VMEM)] + [spec(pltpu.HBM)] * 2,
        scratch_shapes=CLEARING,
        compiler_params=pltpu.CompilerParams(vmem_limit_bytes=4 * MIB),
        cost_estimate=SMALL,
        name="turn",
    )(listed, in_vmem(packed), later_than)


def chip_body(tokens, gate_weight, up_weight, block_mask, cotangent):
    swap = [(0, 1), (1, 0)]
    width = tokens.shape[1]
    columns, segs = gate_weight.shape[1] // BLOCK, gate_weight.shape[0] // BLOCK
    cut = columns // 2
    listed = places(block_mask.T, segs)
    other_cot = lax.ppermute(cotangent, "row", swap)

    again = join(tokens, later_than=other_cot)
    blocks = [
        lax.ppermute(block, AXES, z_pairs(turn, k0)) for turn in range(2) for k0, block in enumerate((tokens, again))
    ]
    (pack_a,) = pack(0, cut, listed, gate_weight, up_weight, other_cot)
    own = join(*blocks, later_than=pack_a)
    near = lax.ppermute(own, AXES, NEAR)
    pack_b, turned_a = pack(cut, columns - cut, listed, gate_weight, up_weight, own, pack_a)
    heres = mix(own, near, later_than=pack_b)
    theres = [lax.ppermute(here, AXES, FAR) for here in heres]
    turned_b, *written = transposed(listed, pack_b, gate_weight.shape, heres[1])
    turned, packed = (turned_a, turned_b), (pack_a, pack_b)

    part_a, toks_a = forward(0, listed, packed, (heres[0], theres[0]), turned_b)
    part_b, toks_b = forward(1, listed, packed, (heres[1], theres[1]), turned_b)
    toks = (toks_a, toks_b)
    other_a, other_b = (lax.ppermute(part, "row", swap) for part in (part_a, part_b))
    shown, grads_a, far_a, near_a = backward(0, listed, turned, part_a, other_a, cotangent, other_cot, width)
    hidden, grads_b, far_b, near_b = backward(1, listed, turned, part_b, other_b, cotangent, other_cot, width, shown)
    grads = (grads_a, grads_b)

    pair = 2 * BLOCK
    got_a = lax.ppermute(far_a, AXES, FAR)
    first_b, direct_b = lax.ppermute(far_b[:pair], AXES, FAR), lax.ppermute(far_b[pair:], AXES, FAR)
    sum_a = add((0, near_a), (0, got_a), later_than=far_b)
    carried_a = lax.ppermute(sum_a, AXES, NEAR)
    sum_b = add((0, near_b), (0, first_b), later_than=sum_a)
    carried_b = lax.ppermute(sum_b, AXES, NEAR)
    here_a = add((pair, near_a), (pair, got_a), (0, carried_a), later_than=sum_b)
    here_b = add((pair, near_b), (0, direct_b), (0, carried_b), later_than=here_a)

    def homeward(turn, here):
        for k0 in range(2):
            back = [(b, a) for a, b in z_pairs(turn, k0)]
            yield lax.ppermute(here[k0 * BLOCK : (k0 + 1) * BLOCK], AXES, back)

    home_a, home_b = list(homeward(0, here_a)), list(homeward(1, here_b))
    joined_a = join(*home_a, later_than=here_b)
    lead = columns * 5 // 6
    written = weight_grads(0, lead, listed, toks, grads, written, here_b)
    written = weight_grads(lead, columns - lead, listed, toks, grads, written, joined_a)
    total = sum(piece.astype(F32) for piece in (joined_a[:BLOCK], joined_a[BLOCK:], *home_b))
    return hidden, total.astype(BF16), *written


def solution(mesh):
    fits = mesh.shape["row"] == ROWS and mesh.shape["col"] == COLS
    placed = (P("row", "col"), P("row", "col"), P("row", "col"), P(None, "col"), P("row", "col"))
    return jax.shard_map(
        chip_body if fits else general_body,
        mesh=mesh,
        in_specs=placed,
        out_specs=(P("row", "col"), P("row", "col"), P("row", "col"), P("row", "col")),
        check_vma=False,
    )
```

```python
import functools

import jax
import jax.numpy as jnp
from jax import lax
from jax.experimental import pallas as pl
from jax.experimental.pallas import tpu as pltpu
from jax.sharding import PartitionSpec as P

BLOCK = 128
MIB = 1 << 20
AXES = ("row", "col")
ROWS, COLS = 2, 16
F32, BF16 = jnp.float32, jnp.bfloat16
VMEM, SMEM = pltpu.VMEM, pltpu.SMEM


def expand_mask(small_mask):
    return jnp.repeat(jnp.repeat(small_mask, BLOCK, axis=0), BLOCK, axis=1)


def general_body(tokens, gate_weight, up_weight, block_mask, cotangent):
    row_groups = lax.axis_size("row")
    row_index = lax.axis_index("row")
    seg_rows = gate_weight.shape[0]
    seg_blocks = seg_rows // BLOCK
    out_columns = gate_weight.shape[1]
    column_blocks = out_columns // BLOCK
    gathered = lax.all_gather(tokens, "col", axis=1, tiled=True)
    mask_groups = block_mask.reshape(row_groups, seg_blocks, column_blocks)
    own_mask = lax.dynamic_index_in_dim(mask_groups, row_index, 0, keepdims=False)
    own_expanded = expand_mask(own_mask).astype(jnp.bfloat16)
    gate_panel, up_panel = (
        lax.all_gather(gate_weight * own_expanded, "row", axis=0, tiled=True),
        lax.all_gather(up_weight * own_expanded, "row", axis=0, tiled=True),
    )
    gate = jnp.dot(gathered, gate_panel, preferred_element_type=jnp.float32)
    up_values = jnp.dot(gathered, up_panel, preferred_element_type=jnp.float32)
    sigmoid_gate = jax.nn.sigmoid(gate)
    silu_gate = gate * sigmoid_gate
    hidden = (silu_gate * up_values).astype(jnp.bfloat16)
    cot_float = cotangent.astype(jnp.float32)
    grad_gate = (cot_float * up_values * sigmoid_gate * (1.0 + gate * (1.0 - sigmoid_gate))).astype(
        jnp.bfloat16
    )
    grad_up = (cot_float * silu_gate).astype(jnp.bfloat16)
    contract = (((1,), (1,)), ((), ()))
    transposed = lax.psum_scatter(
        lax.dot_general(gate_panel, grad_gate, contract, preferred_element_type=jnp.float32)
        + lax.dot_general(up_panel, grad_up, contract, preferred_element_type=jnp.float32),
        "col",
        scatter_dimension=0,
        tiled=True,
    )
    input_grad = transposed.T.astype(jnp.bfloat16)
    token_contract = (((0,), (0,)), ((), ()))
    gate_partial = lax.dot_general(
        gathered, grad_gate, token_contract, preferred_element_type=jnp.float32
    )
    up_partial = lax.dot_general(
        gathered, grad_up, token_contract, preferred_element_type=jnp.float32
    )
    gate_sums, up_sums = (
        lax.psum_scatter(
            gate_partial.astype(jnp.bfloat16), "row", scatter_dimension=0, tiled=True
        ).astype(jnp.float32),
        lax.psum_scatter(
            up_partial.astype(jnp.bfloat16), "row", scatter_dimension=0, tiled=True
        ).astype(jnp.float32),
    )
    mask_float = expand_mask(own_mask).astype(jnp.float32)
    gate_grad = gate_sums * mask_float
    up_grad = up_sums * mask_float
    return (hidden, input_grad, gate_grad, up_grad)


def place(row, z, y, x):
    return row * COLS + z * 4 + y * 2 + x


def z_pairs(k1, k0):
    return [
        (place(k1 ^ (z >> 1), 2 * half + 1 - (k0 ^ (z & 1)), y, x), place(half, z, y, x))
        for half in range(2)
        for z in range(4)
        for y in range(2)
        for x in range(2)
    ]


def lane_pairs(first, second):
    return [(r * COLS + c, r * COLS + (c ^ (first, second)[r])) for r in range(2) for c in range(COLS)]


X, Y = 1, 2
NEAR, FAR, ACROSS = lane_pairs(X, Y), lane_pairs(Y, X), lane_pairs(X + Y, X + Y)
SLACK = 4
SMALL = pl.CostEstimate(flops=1, bytes_accessed=1, transcendentals=0)


def coords():
    row, col = lax.axis_index("row"), lax.axis_index("col")
    return row, col // 4, (col // 2) % 2, col % 2


def flip(bit, with_bit):
    return bit + with_bit - 2 * bit * with_bit


def block_of(q, dnear, dfar, k1, k0):
    row, z, y, x = q
    dy = dnear * row + dfar * (1 - row)
    dx = dnear * (1 - row) + dfar * row
    return flip(1 - k0, z % 2) * 4 + flip(dy, y) * 2 + flip(dx, x), flip(k1, z // 2)


def in_vmem(array):
    return pltpu.with_memory_space_constraint(array, VMEM)


def in_hbm(array):
    return pltpu.with_memory_space_constraint(array, pltpu.HBM)


def spec(space):
    return pl.BlockSpec(memory_space=space)


def spanning(index):
    return pl.ds(pl.multiple_of(index * BLOCK, BLOCK), BLOCK)


def kept_of(listed):
    return listed.shape[1] // 2 - SLACK


def list_kernel(mask, listed):
    columns, half = listed.shape[0], listed.shape[1] // 2
    segs = mask.shape[1] // ROWS
    low = lax.axis_index("row") == 0
    own = jnp.where(low, mask[:, :segs], mask[:, segs:])
    before = lax.broadcasted_iota(jnp.int32, (segs, segs), 0) <= lax.broadcasted_iota(jnp.int32, (segs, segs), 1)
    kept = jnp.dot(own.astype(F32), before.astype(F32), preferred_element_type=F32).astype(jnp.int32)
    dropped = lax.broadcasted_iota(jnp.int32, (columns, segs), 1) + 1 - kept
    lane = lax.broadcasted_iota(jnp.int32, (columns, 2 * half), 1)
    out = jnp.zeros((columns, 2 * half), jnp.int32)
    for counts, first in ((kept, 0), (dropped, half)):
        for k in range(segs // 2):
            place = jnp.sum((counts <= k).astype(jnp.int32), axis=1, keepdims=True)
            out = jnp.where(lane == first + k, place, out)
    listed[...] = out


def places(mask_t, segs):
    return pl.pallas_call(
        list_kernel,
        out_shape=VMEM((mask_t.shape[0], segs + 2 * SLACK), jnp.int32),
        in_specs=[spec(VMEM)],
        out_specs=spec(VMEM),
        compiler_params=pltpu.CompilerParams(vmem_limit_bytes=4 * MIB),
        cost_estimate=SMALL,
        name="places",
    )(mask_t)


def pack_kernel(first, turning, listed, gate_w, up_w, *refs):
    if turning:
        earlier, _, packed, turned, sem = refs
    else:
        _, packed, sem = refs
    columns, kept = packed.shape[0], kept_of(listed)

    def column(j, _):
        cols = spanning(first + j)
        for k in range(kept):
            rows = spanning(listed[first + j, k])
            to = packed.at[j, k * BLOCK : (k + 1) * BLOCK]
            pltpu.make_async_copy(gate_w.at[rows, cols], to.at[:, :BLOCK], sem).start()
            pltpu.make_async_copy(up_w.at[rows, cols], to.at[:, BLOCK:], sem).start()
        return 0

    lax.fori_loop(0, columns, column, 0)
    if turning:

        def turn(j, _):
            turned[j] = earlier[j].T
            return 0

        lax.fori_loop(0, earlier.shape[0], turn, 0)
    pltpu.make_async_copy(packed, packed, sem).wait()


def pack(first, columns, listed, gate_w, up_w, later_than, earlier=None):
    turning = earlier is not None
    outs = [VMEM((columns, kept_of(listed) * BLOCK, 2 * BLOCK), BF16)]
    if turning:
        outs.append(VMEM((earlier.shape[0], earlier.shape[2], earlier.shape[1]), BF16))
    return pl.pallas_call(
        functools.partial(pack_kernel, first, turning),
        out_shape=outs,
        in_specs=[spec(SMEM), spec(pltpu.HBM), spec(pltpu.HBM)] + [spec(VMEM)] * turning + [spec(pl.ANY)],
        out_specs=[spec(VMEM)] * len(outs),
        scratch_shapes=[pltpu.SemaphoreType.DMA],
        compiler_params=pltpu.CompilerParams(vmem_limit_bytes=4 * MIB),
        cost_estimate=SMALL,
        name="pack",
    )(listed, in_hbm(gate_w), in_hbm(up_w), *([in_vmem(earlier)] if turning else []), later_than)


def start_clearing(first, count, listed, zeros, gate_out, up_out, sem):
    zeros[...] = jnp.zeros_like(zeros)
    kept = kept_of(listed)

    def column(j, _):
        cols = spanning(first + j)
        for k in range(kept):
            rows = spanning(listed[first + j, kept + SLACK + k])
            pltpu.make_async_copy(zeros, gate_out.at[rows, cols], sem).start()
            pltpu.make_async_copy(zeros, up_out.at[rows, cols], sem).start()
        return 0

    lax.fori_loop(0, count, column, 0)


def finish_clearing(count, gate_out, sem):
    written = gate_out.at[:, pl.ds(0, count * BLOCK)]
    pltpu.make_async_copy(written, written, sem).wait()


CLEARING = [VMEM((BLOCK, BLOCK), F32), pltpu.SemaphoreType.DMA]


def forward_kernel(turn, listed, packed_a, packed_b, here, there, _, part, turned, tokens):
    q = coords()
    width = here.shape[1] // BLOCK
    for dfar, ref in enumerate((here, there)):
        for slot in range(4):
            chip, _ = block_of(q, slot // 2, dfar, turn, slot % 2)
            for s in range(width):
                tokens[chip * width + s] = ref[slot * BLOCK : (slot + 1) * BLOCK, s * BLOCK : (s + 1) * BLOCK]
    cut = packed_a.shape[0]
    for j in range(part.shape[0]):
        picked = jnp.concatenate([tokens[listed[j, k]] for k in range(kept_of(listed))], axis=1)
        weights = packed_a[j] if j < cut else packed_b[j - cut]
        part[j] = jnp.dot(picked, weights, preferred_element_type=F32)
    for i in range(tokens.shape[0]):
        turned[i] = tokens[i].T


def forward(turn, listed, packed, parts, later_than):
    columns = packed[0].shape[0] + packed[1].shape[0]
    seg = parts[0].shape[1] // BLOCK * 8
    return pl.pallas_call(
        functools.partial(forward_kernel, turn),
        out_shape=[VMEM((columns, BLOCK, 2 * BLOCK), F32), VMEM((seg, BLOCK, BLOCK), BF16)],
        in_specs=[spec(SMEM)] + [spec(VMEM)] * 4 + [spec(pl.ANY)],
        out_specs=[spec(VMEM)] * 2,
        scratch_shapes=[VMEM((seg, BLOCK, BLOCK), BF16)],
        compiler_params=pltpu.CompilerParams(vmem_limit_bytes=8 * MIB),
        cost_estimate=SMALL,
        name="forward",
    )(listed, *map(in_vmem, packed), *parts, later_than)


def backward_kernel(turn, listed, turned_a, turned_b, part, other, cot, other_cot, *refs):
    if turn:
        before, hidden, grads, far, near, acc = refs
    else:
        hidden, grads, far, near, acc = refs
    q = coords()
    columns, kept = part.shape[0], kept_of(listed)
    mine = flip(turn, q[1] // 2) == q[0]
    acc[...] = jnp.zeros_like(acc)
    cut = turned_a.shape[0]

    def column(j, turned, at):
        cols = spanning(j)
        total = part[j] + other[j]
        gate, up = total[:, :BLOCK], total[:, BLOCK:]
        sig = 1.0 / (1.0 + jnp.exp(-gate))
        silu = gate * sig
        cotf = jnp.where(mine, cot[:, cols], other_cot[:, cols]).astype(F32)
        shown = (silu * up).astype(BF16)
        hidden[:, cols] = jnp.where(mine, shown, before[:, cols]) if turn else shown
        grads[j, :, :BLOCK] = (cotf * up * sig * (1.0 + gate * (1.0 - sig))).astype(BF16)
        grads[j, :, BLOCK:] = (cotf * silu).astype(BF16)
        spread = jnp.dot(grads[j], turned[at], preferred_element_type=F32)
        for k in range(kept):
            acc[listed[j, k]] += spread[:, k * BLOCK : (k + 1) * BLOCK]

    step = 4
    for turned, first, number in ((turned_a, 0, cut), (turned_b, cut, columns - cut)):

        def steps(g, _, turned=turned, first=first):
            for u in range(step):
                column(first + g * step + u, turned, g * step + u)
            return 0

        lax.fori_loop(0, number // step, steps, 0)
    width = far.shape[1] // BLOCK
    for dfar, ref in enumerate((near, far)):
        for slot in range(4):
            chip, _ = block_of(q, 1 - slot // 2, dfar, turn, slot % 2)
            for s in range(width):
                ref[slot * BLOCK : (slot + 1) * BLOCK, s * BLOCK : (s + 1) * BLOCK] = acc[chip * width + s].astype(BF16)


def backward(turn, listed, packed, part, other, cot, other_cot, width, before=None):
    columns = part.shape[0]
    extra = [] if before is None else [before]
    return pl.pallas_call(
        functools.partial(backward_kernel, turn),
        out_shape=[VMEM(cot.shape, BF16), VMEM((columns, BLOCK, 2 * BLOCK), BF16)]
        + [VMEM((4 * BLOCK, width), BF16)] * 2,
        in_specs=[spec(SMEM)] + [spec(VMEM)] * (6 + len(extra)),
        out_specs=[spec(VMEM)] * 4,
        scratch_shapes=[VMEM((8 * width // BLOCK, BLOCK, BLOCK), F32)],
        compiler_params=pltpu.CompilerParams(vmem_limit_bytes=8 * MIB),
        cost_estimate=SMALL,
        name="backward",
    )(listed, *map(in_vmem, packed), in_vmem(part), in_vmem(other), cot, other_cot, *extra)


def weight_kernel(first, count, listed, toks0, toks1, grads0, grads1, gate_in, up_in, _, gate_out, up_out, token, stage, sems):
    token[...] = jnp.zeros_like(token)
    kept, slots = kept_of(listed), stage.shape[0]
    for j in range(first, first + count):
        slot = (j - first) % slots
        if j - first >= slots:
            pltpu.make_async_copy(stage.at[slot], stage.at[slot], sems.at[slot]).wait()
        picked = jnp.concatenate(
            [jnp.concatenate([toks0[listed[j, k]], toks1[listed[j, k]]], axis=1) for k in range(kept)], axis=0
        )
        grads = jnp.concatenate([grads0[j], grads1[j]], axis=0)
        stage[slot] = jnp.dot(picked, grads, preferred_element_type=F32)
        for k in range(kept):
            rows = spanning(listed[j, k])
            here = stage.at[slot, k * BLOCK : (k + 1) * BLOCK]
            pltpu.make_async_copy(here.at[:, :BLOCK], gate_out.at[rows, spanning(j)], sems.at[slot]).start()
            pltpu.make_async_copy(here.at[:, BLOCK:], up_out.at[rows, spanning(j)], sems.at[slot]).start()
    for slot in range(slots):
        pltpu.make_async_copy(stage.at[slot], stage.at[slot], sems.at[slot]).wait()


def weight_grads(first, count, listed, tokens, grads, written, later_than):
    slots = min(6, count)
    return pl.pallas_call(
        functools.partial(weight_kernel, first, count),
        out_shape=[pltpu.HBM(grad.shape, F32) for grad in written] + [VMEM((8, BLOCK), F32)],
        in_specs=[spec(SMEM)] + [spec(VMEM)] * 4 + [spec(pltpu.HBM)] * 2 + [spec(pl.ANY)],
        out_specs=[spec(pltpu.HBM)] * 2 + [spec(VMEM)],
        scratch_shapes=[VMEM((slots, kept_of(listed) * BLOCK, 2 * BLOCK), F32), pltpu.SemaphoreType.DMA((slots,))],
        input_output_aliases={5: 0, 6: 1},
        compiler_params=pltpu.CompilerParams(vmem_limit_bytes=16 * MIB),
        cost_estimate=SMALL,
        name="weight_grads",
    )(listed, *map(in_vmem, tokens), *map(in_vmem, grads), *map(in_hbm, written), later_than)


def seal_kernel(written, _, same):
    pass


def seal(written, later_than):
    return pl.pallas_call(
        seal_kernel,
        out_shape=pltpu.HBM(written.shape, F32),
        in_specs=[spec(pltpu.HBM), spec(pl.ANY)],
        out_specs=spec(pltpu.HBM),
        input_output_aliases={0: 0},
        compiler_params=pltpu.CompilerParams(vmem_limit_bytes=4 * MIB),
        cost_estimate=SMALL,
        name="seal",
    )(in_hbm(written), later_than)


def add_kernel(firsts, *refs):
    out = refs[-1]
    total = 0.0
    for first, ref in zip(firsts, refs):
        total += ref[first : first + out.shape[0]].astype(F32)
    out[...] = total.astype(BF16)


def add(*terms, later_than):
    firsts, arrays = zip(*terms)
    return pl.pallas_call(
        functools.partial(add_kernel, firsts),
        out_shape=VMEM((2 * BLOCK, arrays[0].shape[1]), BF16),
        in_specs=[spec(VMEM)] * len(arrays) + [spec(pl.ANY)],
        out_specs=spec(VMEM),
        compiler_params=pltpu.CompilerParams(vmem_limit_bytes=4 * MIB),
        cost_estimate=SMALL,
        name="add",
    )(*arrays, later_than)


def join_kernel(_, *refs):
    ins, out = refs[:-1], refs[-1]
    size = ins[0].shape[0]
    for i, ref in enumerate(ins):
        out[i * size : (i + 1) * size] = ref[...]


def join(*parts, later_than):
    rows, width = parts[0].shape
    return pl.pallas_call(
        join_kernel,
        out_shape=VMEM((len(parts) * rows, width), BF16),
        in_specs=[spec(pl.ANY)] + [spec(VMEM)] * len(parts),
        out_specs=spec(VMEM),
        compiler_params=pltpu.CompilerParams(vmem_limit_bytes=4 * MIB),
        cost_estimate=SMALL,
        name="join",
    )(later_than, *parts)


def mix_kernel(_, own, near, *outs):
    half = own.shape[0] // 2
    for i, out in enumerate(outs):
        out[:half] = own[i * half : (i + 1) * half]
        out[half:] = near[i * half : (i + 1) * half]


def mix(own, near, later_than):
    return pl.pallas_call(
        mix_kernel,
        out_shape=[VMEM(own.shape, BF16)] * 2,
        in_specs=[spec(pl.ANY)] + [spec(VMEM)] * 2,
        out_specs=[spec(VMEM)] * 2,
        compiler_params=pltpu.CompilerParams(vmem_limit_bytes=4 * MIB),
        cost_estimate=SMALL,
        name="mix",
    )(later_than, own, near)


def turn_kernel(listed, packed, _, turned, gate_out, up_out, zeros, sem):
    start_clearing(0, listed.shape[0], listed, zeros, gate_out, up_out, sem)

    def turn(j, _):
        turned[j] = packed[j].T
        return 0

    lax.fori_loop(0, packed.shape[0], turn, 0)
    finish_clearing(listed.shape[0], gate_out, sem)


def transposed(listed, packed, grad_shape, later_than):
    columns, rows, wide = packed.shape
    return pl.pallas_call(
        turn_kernel,
        out_shape=[VMEM((columns, wide, rows), BF16)] + [pltpu.HBM(grad_shape, F32)] * 2,
        in_specs=[spec(SMEM), spec(VMEM), spec(pl.ANY)],
        out_specs=[spec(VMEM)] + [spec(pltpu.HBM)] * 2,
        scratch_shapes=CLEARING,
        compiler_params=pltpu.CompilerParams(vmem_limit_bytes=4 * MIB),
        cost_estimate=SMALL,
        name="turn",
    )(listed, in_vmem(packed), later_than)


def chip_body(tokens, gate_weight, up_weight, block_mask, cotangent):
    swap = [(0, 1), (1, 0)]
    width = tokens.shape[1]
    columns, segs = gate_weight.shape[1] // BLOCK, gate_weight.shape[0] // BLOCK
    cut = columns // 3
    listed = places(block_mask.T, segs)
    other_cot = lax.ppermute(cotangent, "row", swap)

    again = join(tokens, later_than=other_cot)
    blocks = [
        lax.ppermute(block, AXES, z_pairs(turn, k0)) for turn in range(2) for k0, block in enumerate((tokens, again))
    ]
    (pack_a,) = pack(0, cut, listed, gate_weight, up_weight, other_cot)
    own = join(*blocks, later_than=pack_a)
    near = lax.ppermute(own, AXES, NEAR)
    pack_b, turned_a = pack(cut, columns - cut, listed, gate_weight, up_weight, own, pack_a)
    heres = mix(own, near, later_than=pack_b)
    theres = [lax.ppermute(here, AXES, FAR) for here in heres]
    turned_b, *written = transposed(listed, pack_b, gate_weight.shape, heres[1])
    turned, packed = (turned_a, turned_b), (pack_a, pack_b)

    part_a, toks_a = forward(0, listed, packed, (heres[0], theres[0]), turned_b)
    part_b, toks_b = forward(1, listed, packed, (heres[1], theres[1]), turned_b)
    toks = (toks_a, toks_b)
    other_a, other_b = (lax.ppermute(part, "row", swap) for part in (part_a, part_b))
    shown, grads_a, far_a, near_a = backward(0, listed, turned, part_a, other_a, cotangent, other_cot, width)
    hidden, grads_b, far_b, near_b = backward(1, listed, turned, part_b, other_b, cotangent, other_cot, width, shown)
    grads = (grads_a, grads_b)

    pair = 2 * BLOCK
    got_a = lax.ppermute(far_a, AXES, FAR)
    first_b, direct_b = lax.ppermute(far_b[:pair], AXES, FAR), lax.ppermute(far_b[pair:], AXES, FAR)
    lead = columns // 6
    *written, token = weight_grads(0, lead, listed, toks, grads, written, far_b)
    sum_a = add((0, near_a), (0, got_a), later_than=token)
    carried_a = lax.ppermute(sum_a, AXES, NEAR)
    sum_b = add((0, near_b), (0, first_b), later_than=sum_a)
    carried_b = lax.ppermute(sum_b, AXES, NEAR)
    middle = columns // 4
    *written, token = weight_grads(lead, middle, listed, toks, grads, written, sum_b)
    here_a = add((pair, near_a), (pair, got_a), (0, carried_a), later_than=token)
    here_b = add((pair, near_b), (0, direct_b), (0, carried_b), later_than=here_a)

    def homeward(turn, here):
        for k0 in range(2):
            back = [(b, a) for a, b in z_pairs(turn, k0)]
            yield lax.ppermute(here[k0 * BLOCK : (k0 + 1) * BLOCK], AXES, back)

    home_a, home_b = list(homeward(0, here_a)), list(homeward(1, here_b))
    joined_a = join(*home_a, later_than=here_b)
    last = lead + middle
    *written, _ = weight_grads(last, columns - last, listed, toks, grads, written, here_b)
    written[0] = seal(written[0], joined_a)
    total = sum(piece.astype(F32) for piece in (joined_a[:BLOCK], joined_a[BLOCK:], *home_b))
    return hidden, total.astype(BF16), *written


def solution(mesh):
    fits = mesh.shape["row"] == ROWS and mesh.shape["col"] == COLS
    placed = (P("row", "col"), P("row", "col"), P("row", "col"), P(None, "col"), P("row", "col"))
    return jax.shard_map(
        chip_body if fits else general_body,
        mesh=mesh,
        in_specs=placed,
        out_specs=(P("row", "col"), P("row", "col"), P("row", "col"), P("row", "col")),
        check_vma=False,
    )
```

```python
import functools

import jax
import jax.numpy as jnp
from jax import lax
from jax.experimental import pallas as pl
from jax.experimental.pallas import tpu as pltpu
from jax.sharding import PartitionSpec as P

BLOCK = 128
MIB = 1 << 20
AXES = ("row", "col")
ROWS, COLS = 2, 16
F32, BF16 = jnp.float32, jnp.bfloat16
VMEM, SMEM = pltpu.VMEM, pltpu.SMEM


def expand_mask(small_mask):
    return jnp.repeat(jnp.repeat(small_mask, BLOCK, axis=0), BLOCK, axis=1)


def general_body(tokens, gate_weight, up_weight, block_mask, cotangent):
    row_groups = lax.axis_size("row")
    row_index = lax.axis_index("row")
    seg_rows = gate_weight.shape[0]
    seg_blocks = seg_rows // BLOCK
    out_columns = gate_weight.shape[1]
    column_blocks = out_columns // BLOCK
    gathered = lax.all_gather(tokens, "col", axis=1, tiled=True)
    mask_groups = block_mask.reshape(row_groups, seg_blocks, column_blocks)
    own_mask = lax.dynamic_index_in_dim(mask_groups, row_index, 0, keepdims=False)
    own_expanded = expand_mask(own_mask).astype(jnp.bfloat16)
    gate_panel, up_panel = (
        lax.all_gather(gate_weight * own_expanded, "row", axis=0, tiled=True),
        lax.all_gather(up_weight * own_expanded, "row", axis=0, tiled=True),
    )
    gate = jnp.dot(gathered, gate_panel, preferred_element_type=jnp.float32)
    up_values = jnp.dot(gathered, up_panel, preferred_element_type=jnp.float32)
    sigmoid_gate = jax.nn.sigmoid(gate)
    silu_gate = gate * sigmoid_gate
    hidden = (silu_gate * up_values).astype(jnp.bfloat16)
    cot_float = cotangent.astype(jnp.float32)
    grad_gate = (cot_float * up_values * sigmoid_gate * (1.0 + gate * (1.0 - sigmoid_gate))).astype(
        jnp.bfloat16
    )
    grad_up = (cot_float * silu_gate).astype(jnp.bfloat16)
    contract = (((1,), (1,)), ((), ()))
    transposed = lax.psum_scatter(
        lax.dot_general(gate_panel, grad_gate, contract, preferred_element_type=jnp.float32)
        + lax.dot_general(up_panel, grad_up, contract, preferred_element_type=jnp.float32),
        "col",
        scatter_dimension=0,
        tiled=True,
    )
    input_grad = transposed.T.astype(jnp.bfloat16)
    token_contract = (((0,), (0,)), ((), ()))
    gate_partial = lax.dot_general(
        gathered, grad_gate, token_contract, preferred_element_type=jnp.float32
    )
    up_partial = lax.dot_general(
        gathered, grad_up, token_contract, preferred_element_type=jnp.float32
    )
    gate_sums, up_sums = (
        lax.psum_scatter(
            gate_partial.astype(jnp.bfloat16), "row", scatter_dimension=0, tiled=True
        ).astype(jnp.float32),
        lax.psum_scatter(
            up_partial.astype(jnp.bfloat16), "row", scatter_dimension=0, tiled=True
        ).astype(jnp.float32),
    )
    mask_float = expand_mask(own_mask).astype(jnp.float32)
    gate_grad = gate_sums * mask_float
    up_grad = up_sums * mask_float
    return (hidden, input_grad, gate_grad, up_grad)


def place(row, z, y, x):
    return row * COLS + z * 4 + y * 2 + x


def z_pairs(k1, k0):
    return [
        (place(k1 ^ (z >> 1), 2 * half + 1 - (k0 ^ (z & 1)), y, x), place(half, z, y, x))
        for half in range(2)
        for z in range(4)
        for y in range(2)
        for x in range(2)
    ]


def lane_pairs(first, second):
    return [(r * COLS + c, r * COLS + (c ^ (first, second)[r])) for r in range(2) for c in range(COLS)]


X, Y = 1, 2
NEAR, FAR, ACROSS = lane_pairs(X, Y), lane_pairs(Y, X), lane_pairs(X + Y, X + Y)
SLACK = 4
SMALL = pl.CostEstimate(flops=1, bytes_accessed=1, transcendentals=0)


def coords():
    row, col = lax.axis_index("row"), lax.axis_index("col")
    return row, col // 4, (col // 2) % 2, col % 2


def flip(bit, with_bit):
    return bit + with_bit - 2 * bit * with_bit


def block_of(q, dnear, dfar, k1, k0):
    row, z, y, x = q
    dy = dnear * row + dfar * (1 - row)
    dx = dnear * (1 - row) + dfar * row
    return flip(1 - k0, z % 2) * 4 + flip(dy, y) * 2 + flip(dx, x), flip(k1, z // 2)


def in_vmem(array):
    return pltpu.with_memory_space_constraint(array, VMEM)


def in_hbm(array):
    return pltpu.with_memory_space_constraint(array, pltpu.HBM)


def spec(space):
    return pl.BlockSpec(memory_space=space)


def spanning(index):
    return pl.ds(pl.multiple_of(index * BLOCK, BLOCK), BLOCK)


def kept_of(listed):
    return listed.shape[1] // 2 - SLACK


def list_kernel(mask, listed):
    columns, half = listed.shape[0], listed.shape[1] // 2
    segs = mask.shape[1] // ROWS
    low = lax.axis_index("row") == 0
    own = jnp.where(low, mask[:, :segs], mask[:, segs:])
    before = lax.broadcasted_iota(jnp.int32, (segs, segs), 0) <= lax.broadcasted_iota(jnp.int32, (segs, segs), 1)
    kept = jnp.dot(own.astype(F32), before.astype(F32), preferred_element_type=F32).astype(jnp.int32)
    dropped = lax.broadcasted_iota(jnp.int32, (columns, segs), 1) + 1 - kept
    lane = lax.broadcasted_iota(jnp.int32, (columns, 2 * half), 1)
    out = jnp.zeros((columns, 2 * half), jnp.int32)
    for counts, first in ((kept, 0), (dropped, half)):
        for k in range(segs // 2):
            place = jnp.sum((counts <= k).astype(jnp.int32), axis=1, keepdims=True)
            out = jnp.where(lane == first + k, place, out)
    listed[...] = out


def places(mask_t, segs):
    return pl.pallas_call(
        list_kernel,
        out_shape=VMEM((mask_t.shape[0], segs + 2 * SLACK), jnp.int32),
        in_specs=[spec(VMEM)],
        out_specs=spec(VMEM),
        compiler_params=pltpu.CompilerParams(vmem_limit_bytes=4 * MIB),
        cost_estimate=SMALL,
        name="places",
    )(mask_t)


def pack_kernel(first, turning, listed, gate_w, up_w, *refs):
    if turning:
        earlier, _, packed, turned, sem = refs
    else:
        _, packed, sem = refs
    columns, kept = packed.shape[0], kept_of(listed)

    def column(j, _):
        cols = spanning(first + j)
        for k in range(kept):
            rows = spanning(listed[first + j, k])
            to = packed.at[j, k * BLOCK : (k + 1) * BLOCK]
            pltpu.make_async_copy(gate_w.at[rows, cols], to.at[:, :BLOCK], sem).start()
            pltpu.make_async_copy(up_w.at[rows, cols], to.at[:, BLOCK:], sem).start()
        return 0

    lax.fori_loop(0, columns, column, 0)
    if turning:

        def turn(j, _):
            turned[j] = earlier[j].T
            return 0

        lax.fori_loop(0, earlier.shape[0], turn, 0)
    pltpu.make_async_copy(packed, packed, sem).wait()


def pack(first, columns, listed, gate_w, up_w, later_than, earlier=None):
    turning = earlier is not None
    outs = [VMEM((columns, kept_of(listed) * BLOCK, 2 * BLOCK), BF16)]
    if turning:
        outs.append(VMEM((earlier.shape[0], earlier.shape[2], earlier.shape[1]), BF16))
    return pl.pallas_call(
        functools.partial(pack_kernel, first, turning),
        out_shape=outs,
        in_specs=[spec(SMEM), spec(pltpu.HBM), spec(pltpu.HBM)] + [spec(VMEM)] * turning + [spec(pl.ANY)],
        out_specs=[spec(VMEM)] * len(outs),
        scratch_shapes=[pltpu.SemaphoreType.DMA],
        compiler_params=pltpu.CompilerParams(vmem_limit_bytes=4 * MIB),
        cost_estimate=SMALL,
        name="pack",
    )(listed, in_hbm(gate_w), in_hbm(up_w), *([in_vmem(earlier)] if turning else []), later_than)


def start_clearing(first, count, listed, zeros, gate_out, up_out, sem):
    zeros[...] = jnp.zeros_like(zeros)
    kept = kept_of(listed)

    def column(j, _):
        cols = spanning(first + j)
        for k in range(kept):
            rows = spanning(listed[first + j, kept + SLACK + k])
            pltpu.make_async_copy(zeros, gate_out.at[rows, cols], sem).start()
            pltpu.make_async_copy(zeros, up_out.at[rows, cols], sem).start()
        return 0

    lax.fori_loop(0, count, column, 0)


def finish_clearing(count, gate_out, sem):
    written = gate_out.at[:, pl.ds(0, count * BLOCK)]
    pltpu.make_async_copy(written, written, sem).wait()


CLEARING = [VMEM((BLOCK, BLOCK), F32), pltpu.SemaphoreType.DMA]


def forward_kernel(turn, listed, packed_a, packed_b, here, there, _, part, turned, tokens):
    q = coords()
    width = here.shape[1] // BLOCK
    for dfar, ref in enumerate((here, there)):
        for slot in range(4):
            chip, _ = block_of(q, slot // 2, dfar, turn, slot % 2)
            for s in range(width):
                tokens[chip * width + s] = ref[slot * BLOCK : (slot + 1) * BLOCK, s * BLOCK : (s + 1) * BLOCK]
    cut = packed_a.shape[0]
    for j in range(part.shape[0]):
        picked = jnp.concatenate([tokens[listed[j, k]] for k in range(kept_of(listed))], axis=1)
        weights = packed_a[j] if j < cut else packed_b[j - cut]
        part[j] = jnp.dot(picked, weights, preferred_element_type=F32)
    for i in range(tokens.shape[0]):
        turned[i] = tokens[i].T


def forward(turn, listed, packed, parts, later_than):
    columns = packed[0].shape[0] + packed[1].shape[0]
    seg = parts[0].shape[1] // BLOCK * 8
    return pl.pallas_call(
        functools.partial(forward_kernel, turn),
        out_shape=[VMEM((columns, BLOCK, 2 * BLOCK), F32), VMEM((seg, BLOCK, BLOCK), BF16)],
        in_specs=[spec(SMEM)] + [spec(VMEM)] * 4 + [spec(pl.ANY)],
        out_specs=[spec(VMEM)] * 2,
        scratch_shapes=[VMEM((seg, BLOCK, BLOCK), BF16)],
        compiler_params=pltpu.CompilerParams(vmem_limit_bytes=8 * MIB),
        cost_estimate=SMALL,
        name="forward",
    )(listed, *map(in_vmem, packed), *parts, later_than)


def backward_kernel(turn, listed, turned_a, turned_b, part, other, cot, other_cot, *refs):
    if turn:
        before, hidden, grads, far, near, acc = refs
    else:
        hidden, grads, far, near, acc = refs
    q = coords()
    columns, kept = part.shape[0], kept_of(listed)
    mine = flip(turn, q[1] // 2) == q[0]
    acc[...] = jnp.zeros_like(acc)
    cut = turned_a.shape[0]

    def column(j, turned, at):
        cols = spanning(j)
        total = part[j] + other[j]
        gate, up = total[:, :BLOCK], total[:, BLOCK:]
        sig = 1.0 / (1.0 + jnp.exp(-gate))
        silu = gate * sig
        cotf = jnp.where(mine, cot[:, cols], other_cot[:, cols]).astype(F32)
        shown = (silu * up).astype(BF16)
        hidden[:, cols] = jnp.where(mine, shown, before[:, cols]) if turn else shown
        grads[j, :, :BLOCK] = (cotf * up * sig * (1.0 + gate * (1.0 - sig))).astype(BF16)
        grads[j, :, BLOCK:] = (cotf * silu).astype(BF16)
        spread = jnp.dot(grads[j], turned[at], preferred_element_type=F32)
        for k in range(kept):
            acc[listed[j, k]] += spread[:, k * BLOCK : (k + 1) * BLOCK]

    step = 4
    for turned, first, number in ((turned_a, 0, cut), (turned_b, cut, columns - cut)):

        def steps(g, _, turned=turned, first=first):
            for u in range(step):
                column(first + g * step + u, turned, g * step + u)
            return 0

        lax.fori_loop(0, number // step, steps, 0)
    width = far.shape[1] // BLOCK
    for dfar, ref in enumerate((near, far)):
        for slot in range(4):
            chip, _ = block_of(q, 1 - slot // 2, dfar, turn, slot % 2)
            for s in range(width):
                ref[slot * BLOCK : (slot + 1) * BLOCK, s * BLOCK : (s + 1) * BLOCK] = acc[chip * width + s].astype(BF16)


def backward(turn, listed, packed, part, other, cot, other_cot, width, before=None):
    columns = part.shape[0]
    extra = [] if before is None else [before]
    return pl.pallas_call(
        functools.partial(backward_kernel, turn),
        out_shape=[VMEM(cot.shape, BF16), VMEM((columns, BLOCK, 2 * BLOCK), BF16)]
        + [VMEM((4 * BLOCK, width), BF16)] * 2,
        in_specs=[spec(SMEM)] + [spec(VMEM)] * (6 + len(extra)),
        out_specs=[spec(VMEM)] * 4,
        scratch_shapes=[VMEM((8 * width // BLOCK, BLOCK, BLOCK), F32)],
        compiler_params=pltpu.CompilerParams(vmem_limit_bytes=8 * MIB),
        cost_estimate=SMALL,
        name="backward",
    )(listed, *map(in_vmem, packed), in_vmem(part), in_vmem(other), cot, other_cot, *extra)


def weight_kernel(first, count, listed, toks0, toks1, grads0, grads1, gate_in, up_in, _, gate_out, up_out, token, stage, sems, zeros, sem):
    token[...] = jnp.zeros_like(token)
    columns = listed.shape[0]
    early = columns * 3 // 4
    final = first + count == columns
    if final:
        start_clearing(early, columns - early, listed, zeros, gate_out, up_out, sem)
    kept, slots = kept_of(listed), stage.shape[0]
    for j in range(first, first + count):
        slot = (j - first) % slots
        if j - first >= slots:
            pltpu.make_async_copy(stage.at[slot], stage.at[slot], sems.at[slot]).wait()
        picked = jnp.concatenate(
            [jnp.concatenate([toks0[listed[j, k]], toks1[listed[j, k]]], axis=1) for k in range(kept)], axis=0
        )
        grads = jnp.concatenate([grads0[j], grads1[j]], axis=0)
        stage[slot] = jnp.dot(picked, grads, preferred_element_type=F32)
        for k in range(kept):
            rows = spanning(listed[j, k])
            here = stage.at[slot, k * BLOCK : (k + 1) * BLOCK]
            pltpu.make_async_copy(here.at[:, :BLOCK], gate_out.at[rows, spanning(j)], sems.at[slot]).start()
            pltpu.make_async_copy(here.at[:, BLOCK:], up_out.at[rows, spanning(j)], sems.at[slot]).start()
    for slot in range(slots):
        pltpu.make_async_copy(stage.at[slot], stage.at[slot], sems.at[slot]).wait()
    if final:
        finish_clearing(columns - early, gate_out, sem)


def weight_grads(first, count, listed, tokens, grads, written, later_than):
    slots = min(6, count)
    return pl.pallas_call(
        functools.partial(weight_kernel, first, count),
        out_shape=[pltpu.HBM(grad.shape, F32) for grad in written] + [VMEM((8, BLOCK), F32)],
        in_specs=[spec(SMEM)] + [spec(VMEM)] * 4 + [spec(pltpu.HBM)] * 2 + [spec(pl.ANY)],
        out_specs=[spec(pltpu.HBM)] * 2 + [spec(VMEM)],
        scratch_shapes=[VMEM((slots, kept_of(listed) * BLOCK, 2 * BLOCK), F32), pltpu.SemaphoreType.DMA((slots,)), *CLEARING],
        input_output_aliases={5: 0, 6: 1},
        compiler_params=pltpu.CompilerParams(vmem_limit_bytes=16 * MIB),
        cost_estimate=SMALL,
        name="weight_grads",
    )(listed, *map(in_vmem, tokens), *map(in_vmem, grads), *map(in_hbm, written), later_than)


def seal_kernel(written, _, same):
    pass


def seal(written, later_than):
    return pl.pallas_call(
        seal_kernel,
        out_shape=pltpu.HBM(written.shape, F32),
        in_specs=[spec(pltpu.HBM), spec(pl.ANY)],
        out_specs=spec(pltpu.HBM),
        input_output_aliases={0: 0},
        compiler_params=pltpu.CompilerParams(vmem_limit_bytes=4 * MIB),
        cost_estimate=SMALL,
        name="seal",
    )(in_hbm(written), later_than)


def add_kernel(firsts, *refs):
    out = refs[-1]
    total = 0.0
    for first, ref in zip(firsts, refs):
        total += ref[first : first + out.shape[0]].astype(F32)
    out[...] = total.astype(BF16)


def add(*terms, later_than):
    firsts, arrays = zip(*terms)
    return pl.pallas_call(
        functools.partial(add_kernel, firsts),
        out_shape=VMEM((2 * BLOCK, arrays[0].shape[1]), BF16),
        in_specs=[spec(VMEM)] * len(arrays) + [spec(pl.ANY)],
        out_specs=spec(VMEM),
        compiler_params=pltpu.CompilerParams(vmem_limit_bytes=4 * MIB),
        cost_estimate=SMALL,
        name="add",
    )(*arrays, later_than)


def join_kernel(_, *refs):
    ins, out = refs[:-1], refs[-1]
    size = ins[0].shape[0]
    for i, ref in enumerate(ins):
        out[i * size : (i + 1) * size] = ref[...]


def join(*parts, later_than):
    rows, width = parts[0].shape
    return pl.pallas_call(
        join_kernel,
        out_shape=VMEM((len(parts) * rows, width), BF16),
        in_specs=[spec(pl.ANY)] + [spec(VMEM)] * len(parts),
        out_specs=spec(VMEM),
        compiler_params=pltpu.CompilerParams(vmem_limit_bytes=4 * MIB),
        cost_estimate=SMALL,
        name="join",
    )(later_than, *parts)


def mix_kernel(_, own, near, *outs):
    half = own.shape[0] // 2
    for i, out in enumerate(outs):
        out[:half] = own[i * half : (i + 1) * half]
        out[half:] = near[i * half : (i + 1) * half]


def mix(own, near, later_than):
    return pl.pallas_call(
        mix_kernel,
        out_shape=[VMEM(own.shape, BF16)] * 2,
        in_specs=[spec(pl.ANY)] + [spec(VMEM)] * 2,
        out_specs=[spec(VMEM)] * 2,
        compiler_params=pltpu.CompilerParams(vmem_limit_bytes=4 * MIB),
        cost_estimate=SMALL,
        name="mix",
    )(later_than, own, near)


def turn_kernel(listed, packed, _, turned, gate_out, up_out, zeros, sem):
    early = listed.shape[0] * 3 // 4
    start_clearing(0, early, listed, zeros, gate_out, up_out, sem)

    def turn(j, _):
        turned[j] = packed[j].T
        return 0

    lax.fori_loop(0, packed.shape[0], turn, 0)
    finish_clearing(early, gate_out, sem)


def transposed(listed, packed, grad_shape, later_than):
    columns, rows, wide = packed.shape
    return pl.pallas_call(
        turn_kernel,
        out_shape=[VMEM((columns, wide, rows), BF16)] + [pltpu.HBM(grad_shape, F32)] * 2,
        in_specs=[spec(SMEM), spec(VMEM), spec(pl.ANY)],
        out_specs=[spec(VMEM)] + [spec(pltpu.HBM)] * 2,
        scratch_shapes=CLEARING,
        compiler_params=pltpu.CompilerParams(vmem_limit_bytes=4 * MIB),
        cost_estimate=SMALL,
        name="turn",
    )(listed, in_vmem(packed), later_than)


def chip_body(tokens, gate_weight, up_weight, block_mask, cotangent):
    swap = [(0, 1), (1, 0)]
    width = tokens.shape[1]
    columns, segs = gate_weight.shape[1] // BLOCK, gate_weight.shape[0] // BLOCK
    cut = columns // 3
    listed = places(block_mask.T, segs)
    other_cot = lax.ppermute(cotangent, "row", swap)

    again = join(tokens, later_than=other_cot)
    blocks = [
        lax.ppermute(block, AXES, z_pairs(turn, k0)) for turn in range(2) for k0, block in enumerate((tokens, again))
    ]
    (pack_a,) = pack(0, cut, listed, gate_weight, up_weight, other_cot)
    own = join(*blocks, later_than=pack_a)
    near = lax.ppermute(own, AXES, NEAR)
    pack_b, turned_a = pack(cut, columns - cut, listed, gate_weight, up_weight, own, pack_a)
    heres = mix(own, near, later_than=pack_b)
    theres = [lax.ppermute(here, AXES, FAR) for here in heres]
    turned_b, *written = transposed(listed, pack_b, gate_weight.shape, heres[1])
    turned, packed = (turned_a, turned_b), (pack_a, pack_b)

    part_a, toks_a = forward(0, listed, packed, (heres[0], theres[0]), turned_b)
    part_b, toks_b = forward(1, listed, packed, (heres[1], theres[1]), turned_b)
    toks = (toks_a, toks_b)
    other_a, other_b = (lax.ppermute(part, "row", swap) for part in (part_a, part_b))
    shown, grads_a, far_a, near_a = backward(0, listed, turned, part_a, other_a, cotangent, other_cot, width)
    hidden, grads_b, far_b, near_b = backward(1, listed, turned, part_b, other_b, cotangent, other_cot, width, shown)
    grads = (grads_a, grads_b)

    pair = 2 * BLOCK
    got_a = lax.ppermute(far_a, AXES, FAR)
    first_b, direct_b = lax.ppermute(far_b[:pair], AXES, FAR), lax.ppermute(far_b[pair:], AXES, FAR)
    lead = columns // 6
    *written, token = weight_grads(0, lead, listed, toks, grads, written, far_b)
    sum_a = add((0, near_a), (0, got_a), later_than=token)
    carried_a = lax.ppermute(sum_a, AXES, NEAR)
    sum_b = add((0, near_b), (0, first_b), later_than=sum_a)
    carried_b = lax.ppermute(sum_b, AXES, NEAR)
    middle = columns // 4
    *written, token = weight_grads(lead, middle, listed, toks, grads, written, sum_b)
    here_a = add((pair, near_a), (pair, got_a), (0, carried_a), later_than=token)
    here_b = add((pair, near_b), (0, direct_b), (0, carried_b), later_than=here_a)

    def homeward(turn, here):
        for k0 in range(2):
            back = [(b, a) for a, b in z_pairs(turn, k0)]
            yield lax.ppermute(here[k0 * BLOCK : (k0 + 1) * BLOCK], AXES, back)

    home_a, home_b = list(homeward(0, here_a)), list(homeward(1, here_b))
    joined_a = join(*home_a, later_than=here_b)
    last = lead + middle
    *written, _ = weight_grads(last, columns - last, listed, toks, grads, written, here_b)
    written[0] = seal(written[0], joined_a)
    total = sum(piece.astype(F32) for piece in (joined_a[:BLOCK], joined_a[BLOCK:], *home_b))
    return hidden, total.astype(BF16), *written


def solution(mesh):
    fits = mesh.shape["row"] == ROWS and mesh.shape["col"] == COLS
    placed = (P("row", "col"), P("row", "col"), P("row", "col"), P(None, "col"), P("row", "col"))
    return jax.shard_map(
        chip_body if fits else general_body,
        mesh=mesh,
        in_specs=placed,
        out_specs=(P("row", "col"), P("row", "col"), P("row", "col"), P("row", "col")),
        check_vma=False,
    )
```
